32 devices in a mesh: section: 4 (over z), dp: 8 (over y, x, core).
Axes of the slice: x: 2, y: 2, z: 4, core: 2. Of those that a mesh axis runs over, the one named last changes fastest.
Arguments:
- images: bfloat16 [2, 1576, 1024], P(None, 'dp'), may hold values from -44 to 44
- cotangent: bfloat16 [2, 1576, 1024], P(None, 'dp'), may hold values from -0.75 to 0.75
- w_in: bfloat16 [4, 1024, 2048], P('section'), may hold values from -0.1875 to 0.1875
- w_out: bfloat16 [4, 2048, 1024], P('section'), may hold values from -0.125 to 0.125
- gain: float32 [4, 1024], P('section'), may hold values from 0.5 to 1.5
- shift: float32 [4, 1024], P('section'), may hold values from -3 to 3
Outputs:
- section_outputs: bfloat16 [4, 2, 1576, 1024], P('section', None, 'dp')
- input_grads: bfloat16 [4, 2, 1576, 1024], P('section', None, 'dp')
- grad_w_in: float32 [4, 1024, 2048], P('section', 'dp')
- grad_w_out: float32 [4, 2048, 1024], P('section', 'dp')
- grad_gain: float32 [4, 1024], P('section')
- grad_shift: float32 [4, 1024], P('section')
The draws below stay inside these ranges and needn't reach their ends.
All inputs are finite; a program needn't handle non-finite values.
Results may differ from the reference program's by a relative error of at most 0.0095.
Values may be sent and summed in bfloat16 or wider, within the bound.
A program may use at most 192 MiB of HBM per device.

```python
import jax
import jax.numpy as jnp
from jax import lax

D = 1024
FF = 2048
PATCHES = 197
IMG = 1
MICRO = 2
TOKENS = 1576
SECTIONS = 4
N_DP = 8


def draw_images(key, part):
    keys = jax.random.split(jax.random.fold_in(key, 11), 2)
    positions = jnp.arange(TOKENS)
    block = (positions // (IMG * PATCHES)).astype(jnp.float32)
    spread = max(N_DP - 1, 1)
    centre = jnp.clip(0.5 * jax.random.normal(keys[1], (D,), jnp.float32), -2.0, 2.0)
    noise = jnp.clip(jax.random.normal(keys[0], (MICRO, TOKENS, D), jnp.float32), -4.0, 4.0)
    level = 1.0 + 2.0 * block / spread
    column = jnp.ones((D,), jnp.float32)
    values = centre + level[None, :, None] * column * noise
    return values.astype(jnp.bfloat16)


def raised(entries, key, source, target, blocks, factor):
    owner, partner = [(jnp.arange(entries.shape[position]) // (entries.shape[position] // blocks)).reshape([-1 if axis == position else 1 for axis in range(entries.ndim)]) for position in (source, target)]
    chosen = jax.random.permutation(key, blocks)[partner]
    strong = (owner == chosen) | (owner == (partner + blocks // 2) % blocks)
    return jnp.where(strong, factor * entries, entries)


def block_levels(stream_key, extent, cuts, low, high):
    level, own = 1.0, jax.random.fold_in(stream_key, 6)
    for dim, shards_of in cuts:
        heights = jnp.exp(jax.random.uniform(jax.random.fold_in(own, dim), (shards_of,), jnp.float32, low / len(cuts), high / len(cuts)))
        level = level * jnp.repeat(heights, extent[dim] // shards_of).reshape([-1 if axis == dim else 1 for axis in range(len(extent))])
    return level


def bell_draw(stream_key, shape, scale, most, shards=(), dtype=jnp.bfloat16):
    drawn = jax.random.normal(stream_key, shape, jnp.float32) * scale
    if len(shards) > 0:
        drawn = block_levels(stream_key, shape, shards, -0.22, 0.18) * drawn
    return jnp.clip(drawn, min=-most, max=most).astype(dtype)


def bell_draw_with(key, shape, scale, most, pieces, heavy, held_as=jnp.bfloat16):
    result = scale * jax.random.normal(key, shape, jnp.float32)
    if pieces:
        result = result * block_levels(key, shape, pieces, -0.22, 0.18)
    return jnp.clip(raised(result, jax.random.fold_in(key, 3), *heavy), -most, most).astype(held_as)


def setup_inputs(seed: int = 0) -> dict:
    key_of = jax.random.split(jax.random.key(seed), 7)
    images = draw_images(jax.random.fold_in(key_of[6], 71), 0)
    cotangent = bell_draw_with(key_of[1], (MICRO, TOKENS, D), 0.125, 0.75, ((1, 8),), (1, 2, 8, 2.0))
    w_in = bell_draw(key_of[2], (SECTIONS, D, FF), D ** -0.5, 0.1875, ((0, 4),))
    w_out = bell_draw(key_of[3], (SECTIONS, FF, D), FF ** -0.5, 0.125, ((0, 4),))
    gain = jnp.clip(1.0 + 0.1 * jax.random.normal(key_of[4], (SECTIONS, D), jnp.float32), 0.5, 1.5)
    shift = bell_draw(key_of[5], (SECTIONS, D), 0.5, 3.0, ((0, 4),), jnp.float32)
    return dict(images=images, cotangent=cotangent, w_in=w_in, w_out=w_out, gain=gain, shift=shift)


epsilon = 1e-05
gelu_scale = 0.7978845608028654
cubic_term = 0.044715

def gelu_parts(before):
    inner = gelu_scale * (before + cubic_term * before * before * before)
    bend = jnp.tanh(inner)
    value = 0.5 * before * (1.0 + bend)
    slope = 0.5 * (1.0 + bend) + 0.5 * before * (1.0 - bend * bend) * gelu_scale * (1.0 + 3.0 * cubic_term * before * before)
    return (value, slope)

def reference(images, cotangent, w_in, w_out, gain, shift):
    sections = w_in.shape[0]
    micro = images.shape[0]
    rows = images.shape[1]
    outputs = [[None] * micro for layer in range(sections)]
    in_grads = [[None] * micro for layer in range(sections)]
    stored = {}
    for batch in range(micro):
        inputs = images[batch]
        for layer in range(sections):
            inputs_f = inputs.astype(jnp.float32)
            mean = lax.optimization_barrier(jnp.sum(inputs_f, axis=0)) / rows
            centered = inputs_f - mean
            spread = lax.optimization_barrier(jnp.sum(centered * centered, axis=0)) / rows
            inverse = lax.rsqrt(spread + epsilon)
            normed = centered * inverse
            affine = (normed * gain[layer] + shift[layer]).astype(jnp.bfloat16)
            before = jnp.dot(affine, w_in[layer], preferred_element_type=jnp.float32)
            value, slope = gelu_parts(before)
            active = value.astype(jnp.bfloat16)
            output = (inputs_f + jnp.dot(active, w_out[layer], preferred_element_type=jnp.float32)).astype(jnp.bfloat16)
            stored[layer, batch] = (normed, inverse, affine, slope, active)
            outputs[layer][batch] = output
            inputs = output
    grad_in = [jnp.zeros(w_in.shape[1:], jnp.float32) for layer in range(sections)]
    grad_out = [jnp.zeros(w_out.shape[1:], jnp.float32) for layer in range(sections)]
    grad_gain = [jnp.zeros(gain.shape[1:], jnp.float32) for layer in range(sections)]
    grad_shift = [jnp.zeros(gain.shape[1:], jnp.float32) for layer in range(sections)]
    for batch in range(micro):
        upstream = cotangent[batch]
        for layer in reversed(range(sections)):
            normed, inverse, affine, slope, active = stored[layer, batch]
            grad_out[layer] = grad_out[layer] + jnp.dot(active.T, upstream, preferred_element_type=jnp.float32)
            grad_active = jnp.dot(upstream, w_out[layer].T, preferred_element_type=jnp.float32)
            grad_before = (grad_active * slope).astype(jnp.bfloat16)
            grad_in[layer] = grad_in[layer] + jnp.dot(affine.T, grad_before, preferred_element_type=jnp.float32)
            grad_affine = jnp.dot(grad_before, w_in[layer].T, preferred_element_type=jnp.float32)
            sum_grad = lax.optimization_barrier(jnp.sum(grad_affine, axis=0))
            sum_cross = lax.optimization_barrier(jnp.sum(grad_affine * normed, axis=0))
            grad_gain[layer] = grad_gain[layer] + sum_cross
            grad_shift[layer] = grad_shift[layer] + sum_grad
            grad_norm = inverse * gain[layer] * (grad_affine - sum_grad / rows - normed * sum_cross / rows)
            upstream = (upstream.astype(jnp.float32) + grad_norm).astype(jnp.bfloat16)
            in_grads[layer][batch] = upstream
    section_outputs = jnp.stack([jnp.stack(column) for column in outputs])
    input_grads = jnp.stack([jnp.stack(column) for column in in_grads])
    return (section_outputs, input_grads, jnp.stack(grad_in), jnp.stack(grad_out), jnp.stack(grad_gain), jnp.stack(grad_shift))
```

```python
import functools

import jax
import jax.numpy as jnp
from jax import lax
from jax.experimental import pallas as pl
from jax.experimental.pallas import tpu as pltpu
from jax.sharding import PartitionSpec as P

epsilon = 1e-05
gelu_scale = 0.7978845608028654
cubic_term = 0.044715
f32 = jnp.float32
bf16 = jnp.bfloat16
MESH = pl.DeviceIdType.MESH


def near_square(count):
    side = int(count**0.5)
    while count % side:
        side -= 1
    return side


def loop(count, body):
    def step(i, carry):
        body(i)
        return carry

    lax.fori_loop(0, count, step, 0)


def cut(j, size):
    return pl.ds(pl.multiple_of(j * size, size), size)


def across(lhs, rhs):
    return lax.dot_general(lhs, rhs, (((1,), (1,)), ((), ())), preferred_element_type=f32)


def kernel(
    sizes,
    images, cotangent, w_in, w_out, gain, shift,
    out, gin, red_in, red_out, ggain, gshift,
    xbuf, ubuf, stat, stat_out, ex, aff, active, slope, gb, ga_buf, act_t, aff_t,
    send_i, keep_i, r0_i, r1_i, r2_i,
    send_o, keep_o, r0_o, r1_o, r2_o,
    x_send, x_recv, u_send, u_recv, st_send, st_recv, ex_send, ex_recv,
    s0, q0, s1, q1, s2, q2,
):
    sections, n, micro, real, rp, width, hidden, nx, ny = sizes
    rows = real * n
    wt = min(256, width)
    ht = min(512, hidden)
    nw = width // wt
    nh = hidden // ht
    section = lax.axis_index("section")
    me = lax.axis_index("dp")
    first = section == 0
    last = section == sections - 1
    not_first = section > 0
    not_last = section < sections - 1

    barrier = pltpu.get_barrier_semaphore()

    def greet(k):
        pl.semaphore_signal(
            barrier, inc=1, device_id={"dp": lax.rem(me + k + 1, n)}, device_id_type=MESH
        )

    loop(n - 1, greet)

    @pl.when(not_first)
    def _():
        pl.semaphore_signal(barrier, inc=1, device_id={"section": section - 1}, device_id_type=MESH)

    @pl.when(not_last)
    def _():
        pl.semaphore_signal(barrier, inc=1, device_id={"section": section + 1}, device_id_type=MESH)

    peers = n - 1 + not_first.astype(jnp.int32) + not_last.astype(jnp.int32)
    pl.semaphore_wait(barrier, peers)

    valid = lax.broadcasted_iota(jnp.int32, (rp, wt), 0) < real

    def local_stats(kind, m, j, tile):
        mean = jnp.sum(tile, axis=0, keepdims=True) / real
        gap = jnp.where(valid, tile - mean, 0.0)
        ex[kind, m, me, 0:1, cut(j, wt)] = mean
        ex[kind, m, me, 1:2, cut(j, wt)] = jnp.sum(gap * gap, axis=0, keepdims=True)

    def ex_copy(kind, m, k, slot):
        return pltpu.make_async_remote_copy(
            src_ref=ex.at[kind, m, slot],
            dst_ref=ex.at[kind, m, slot],
            send_sem=ex_send.at[kind, m, k],
            recv_sem=ex_recv.at[kind, m, k],
            device_id={"dp": lax.rem(me + k + 1, n)},
            device_id_type=MESH,
        )

    def ex_start(kind, m):
        loop(n - 1, lambda k: ex_copy(kind, m, k, me).start())

    def ex_wait(kind, m):
        loop(n - 1, lambda k: ex_copy(kind, m, k, lax.rem(me - k - 1 + n, n)).wait_recv())
        loop(n - 1, lambda k: ex_copy(kind, m, k, me).wait_send())
        return ex[kind, m]

    def combine(kind, m, target):
        parts = ex_wait(kind, m)
        means = parts[:, 0, :]
        mean = jnp.sum(means, axis=0, keepdims=True) / n
        gap = means - mean
        spread = (
            jnp.sum(parts[:, 1, :], axis=0, keepdims=True)
            + real * jnp.sum(gap * gap, axis=0, keepdims=True)
        ) / rows
        target[m, 0:1, :] = mean
        target[m, 1:2, :] = lax.rsqrt(spread + epsilon)

    def x_copy(m, j):
        return pltpu.make_async_remote_copy(
            src_ref=out.at[0, m, :, cut(j, wt)],
            dst_ref=xbuf.at[m, :, cut(j, wt)],
            send_sem=x_send.at[m, j],
            recv_sem=x_recv.at[m, j],
            device_id={"section": section + 1},
            device_id_type=MESH,
        )

    def u_copy(m, j):
        return pltpu.make_async_remote_copy(
            src_ref=gin.at[0, m, :, cut(j, wt)],
            dst_ref=ubuf.at[m, :, cut(j, wt)],
            send_sem=u_send.at[m, j],
            recv_sem=u_recv.at[m, j],
            device_id={"section": section - 1},
            device_id_type=MESH,
        )

    def st_copy(m):
        return pltpu.make_async_remote_copy(
            src_ref=stat_out.at[m],
            dst_ref=stat.at[m],
            send_sem=st_send.at[m],
            recv_sem=st_recv.at[m],
            device_id={"section": section + 1},
            device_id_type=MESH,
        )

    ggain[...] = jnp.zeros_like(ggain)
    gshift[...] = jnp.zeros_like(gshift)

    @pl.when(first)
    def _():
        for m in range(micro):
            xbuf[m, rp - 16 : rp, :] = jnp.zeros((16, width), bf16)
            xbuf[m, 0:real, :] = images[m]

            def tile(j):
                local_stats(0, m, j, xbuf[m, :, cut(j, wt)].astype(f32))

            loop(nw, tile)
            ex_start(0, m)
        for m in range(micro):
            combine(0, m, stat)

    @pl.when(last)
    def _():
        for m in range(micro):
            ubuf[m, rp - 16 : rp, :] = jnp.zeros((16, width), bf16)
            ubuf[m, 0:real, :] = cotangent[m]

    def forward(m):
        @pl.when(not_first)
        def _():
            loop(nw, lambda j: x_copy(m, j).wait_recv())
            st_copy(m).wait_recv()

        mean = stat[m, 0:1, :]
        inverse = stat[m, 1:2, :]
        aff[m] = (
            (xbuf[m].astype(f32) - mean) * inverse * gain[...] + shift[...]
        ).astype(bf16)

        def hidden_tile(j):
            before = jnp.dot(aff[m], w_in[0, :, cut(j, ht)], preferred_element_type=f32)
            bend = jnp.tanh(gelu_scale * (before + cubic_term * before * before * before))
            active[m, :, cut(j, ht)] = (0.5 * before * (1.0 + bend)).astype(bf16)
            slope[m, :, cut(j, ht)] = before

        loop(nh, hidden_tile)

        def out_tile(j):
            fresh = xbuf[m, :, cut(j, wt)].astype(f32) + jnp.dot(
                active[m], w_out[0, :, cut(j, wt)], preferred_element_type=f32
            )
            fresh = jnp.where(valid, fresh, 0.0).astype(bf16)
            out[0, m, :, cut(j, wt)] = fresh

            @pl.when(not_last)
            def _():
                x_copy(m, j).start()
                local_stats(1, m, j, fresh.astype(f32))

        loop(nw, out_tile)

        @pl.when(not_last)
        def _():
            ex_start(1, m)
            combine(1, m, stat_out)
            st_copy(m).start()

        def tail_tile(j):
            before = slope[m, :, cut(j, ht)]
            bend = jnp.tanh(gelu_scale * (before + cubic_term * before * before * before))
            slope[m, :, cut(j, ht)] = 0.5 * (1.0 + bend) + 0.5 * before * (
                1.0 - bend * bend
            ) * gelu_scale * (1.0 + 3.0 * cubic_term * before * before)
            act_t[m, cut(j, ht), :] = active[m, :, cut(j, ht)].T

        loop(nh, tail_tile)

        def turn_tile(j):
            aff_t[m, cut(j, wt), :] = aff[m, :, cut(j, wt)].T

        loop(nw, turn_tile)

    def backward(m):
        @pl.when(not_last)
        def _():
            loop(nw, lambda j: u_copy(m, j).wait_recv())

        def hidden_tile(j):
            pulled = across(ubuf[m], w_out[0, cut(j, ht), :])
            gb[m, :, cut(j, ht)] = (pulled * slope[m, :, cut(j, ht)]).astype(bf16)

        loop(nh, hidden_tile)

        def normed_of(j):
            return (
                xbuf[m, :, cut(j, wt)].astype(f32) - stat[m, 0:1, cut(j, wt)]
            ) * stat[m, 1:2, cut(j, wt)]

        def affine_tile(j):
            pulled = across(gb[m], w_in[0, cut(j, wt), :])
            ga_buf[:, cut(j, wt)] = pulled
            ex[2, m, me, 0:1, cut(j, wt)] = jnp.sum(pulled, axis=0, keepdims=True)
            ex[2, m, me, 1:2, cut(j, wt)] = jnp.sum(pulled * normed_of(j), axis=0, keepdims=True)

        loop(nw, affine_tile)
        ex_start(2, m)
        parts = ex_wait(2, m)
        ggain[...] += jnp.sum(parts[:, 1, :], axis=0, keepdims=True)
        gshift[...] += jnp.sum(parts[:, 0, :], axis=0, keepdims=True)

        def grad_tile(j):
            cols = cut(j, wt)
            sums = ex[2, m, :, :, cols]
            sum_grad = jnp.sum(sums[:, 0, :], axis=0, keepdims=True)
            sum_cross = jnp.sum(sums[:, 1, :], axis=0, keepdims=True)
            normed = normed_of(j)
            fresh = ubuf[m, :, cols].astype(f32) + stat[m, 1:2, cols] * gain[:, cols] * (
                ga_buf[:, cols] - sum_grad / rows - normed * (sum_cross / rows)
            )
            gin[0, m, :, cols] = jnp.where(valid, fresh, 0.0).astype(bf16)

            @pl.when(not_first)
            def _():
                u_copy(m, j).start()

        loop(nw, grad_tile)

    def step(t):
        ahead = jnp.where(last, lax.rem(t, 2) == 0, t < micro)
        m = jnp.where(last, t // 2, lax.rem(t, micro))

        @pl.when(ahead)
        def _():
            forward(m)

        @pl.when(jnp.logical_not(ahead))
        def _():
            backward(m)

    loop(2 * micro, step)

    core = lax.rem(me, 2)
    chip = me // 2
    my_y = chip // nx
    my_x = lax.rem(chip, nx)

    def place(y, x, c):
        return (y * nx + x) * 2 + c

    plans = (
        (0, ny, nx, my_y, my_x, lambda a, b, c: place(a, b, c), act_t, ubuf,
         send_o, keep_o, r0_o, r1_o, r2_o, red_out, hidden // n),
        (1, nx, ny, my_x, my_y, lambda a, b, c: place(b, a, c), aff_t, gb,
         send_i, keep_i, r0_i, r1_i, r2_i, red_in, width // n),
    )

    def copy0(g, plan, s):
        return pltpu.make_async_remote_copy(
            src_ref=plan[8].at[s], dst_ref=plan[10].at[s],
            send_sem=s0.at[g, s], recv_sem=q0.at[g, s],
            device_id={"dp": chip * 2 + 1 - core}, device_id_type=MESH,
        )

    def copy1(g, plan, k, slot):
        na, nb, a, b, where = plan[1:6]
        to = lax.rem(a + k + 1, na)
        return pltpu.make_async_remote_copy(
            src_ref=plan[8].at[pl.ds(to * nb, nb)], dst_ref=plan[11].at[k],
            send_sem=s1.at[g, k], recv_sem=q1.at[g, k],
            device_id={"dp": where(to, b, core)}, device_id_type=MESH,
        )

    def copy2(g, plan, k):
        na, nb, a, b, where = plan[1:6]
        to = lax.rem(b + k + 1, nb)
        return pltpu.make_async_remote_copy(
            src_ref=plan[8].at[a * nb + to], dst_ref=plan[12].at[k],
            send_sem=s2.at[g, k], recv_sem=q2.at[g, k],
            device_id={"dp": where(a, to, core)}, device_id_type=MESH,
        )

    for plan in plans:
        g, na, nb, a, b, where, left, right, send, keep, r0, r1, r2, red, block = plan

        def partial(owner):
            total = jnp.dot(left[0, cut(owner, block), :], right[0], preferred_element_type=f32)
            for m in range(1, micro):
                total += jnp.dot(left[m, cut(owner, block), :], right[m], preferred_element_type=f32)
            return total

        def away(s):
            send[s] = partial(where(s // nb, lax.rem(s, nb), 1 - core)).astype(bf16)
            copy0(g, plan, s).start()

        loop(na * nb, away)

    for plan in plans:
        g, na, nb, a, b, where, left, right, send, keep, r0, r1, r2, red, block = plan

        def partial(owner):
            total = jnp.dot(left[0, cut(owner, block), :], right[0], preferred_element_type=f32)
            for m in range(1, micro):
                total += jnp.dot(left[m, cut(owner, block), :], right[m], preferred_element_type=f32)
            return total

        def other(k):
            to = lax.rem(a + k + 1, na)

            def one(i):
                s = to * nb + i
                copy0(g, plan, s).wait()
                total = partial(where(to, i, core)) + r0[s].astype(f32)
                send[s] = total.astype(bf16)

            loop(nb, one)
            copy1(g, plan, k, 0).start()

        loop(na - 1, other)

        def own(i):
            s = a * nb + i
            copy0(g, plan, s).wait()
            keep[i] = partial(where(a, i, core)) + r0[s].astype(f32)

        loop(nb, own)

    for plan in plans:
        g, na, nb, a, b, where, left, right, send, keep, r0, r1, r2, red, block = plan
        loop(na - 1, lambda k: copy1(g, plan, k, 0).wait())

        def across_sum(to):
            total = keep[to]
            for k in range(na - 1):
                total += r1[k, to].astype(f32)
            return total

        def other2(k):
            to = lax.rem(b + k + 1, nb)
            send[a * nb + to] = across_sum(to).astype(bf16)
            copy2(g, plan, k).start()

        loop(nb - 1, other2)
        keep[b] = across_sum(b)

    for plan in plans:
        g, na, nb, a, b, where, left, right, send, keep, r0, r1, r2, red, block = plan
        loop(nb - 1, lambda k: copy2(g, plan, k).wait())
        total = keep[b]
        for k in range(nb - 1):
            total += r2[k].astype(f32)
        red[0] = total

    @pl.when(not_last)
    def _():
        for m in range(micro):
            loop(nw, lambda j: x_copy(m, j).wait_send())
            st_copy(m).wait_send()

    @pl.when(not_first)
    def _():
        for m in range(micro):
            loop(nw, lambda j: u_copy(m, j).wait_send())


def local(images, cotangent, w_in, w_out, gain, shift):
    sections = lax.axis_size("section")
    n = lax.axis_size("dp")
    micro, real, width = images.shape
    hidden = w_in.shape[2]
    rp = -(-real // 16) * 16
    chips = n // 2
    ny = near_square(chips)
    nx = chips // ny
    nw = width // min(256, width)
    bi, bo = width // n, hidden // n
    top = max(nx, ny)
    sizes = (sections, n, micro, real, rp, width, hidden, nx, ny)
    shape = jax.ShapeDtypeStruct
    vmem = pl.BlockSpec(memory_space=pltpu.VMEM)
    dma = pltpu.SemaphoreType.DMA
    scratch = [
        pltpu.VMEM((micro, rp, width), bf16),
        pltpu.VMEM((micro, rp, width), bf16),
        pltpu.VMEM((micro, 2, width), f32),
        pltpu.VMEM((micro, 2, width), f32),
        pltpu.VMEM((3, micro, n, 2, width), f32),
        pltpu.VMEM((micro, rp, width), bf16),
        pltpu.VMEM((micro, rp, hidden), bf16),
        pltpu.VMEM((micro, rp, hidden), f32),
        pltpu.VMEM((micro, rp, hidden), bf16),
        pltpu.VMEM((rp, width), f32),
        pltpu.VMEM((micro, hidden, rp), bf16),
        pltpu.VMEM((micro, width, rp), bf16),
    ]
    for na, nb, block, cols in ((nx, ny, bi, hidden), (ny, nx, bo, width)):
        scratch += [
            pltpu.VMEM((chips, block, cols), bf16),
            pltpu.VMEM((nb, block, cols), f32),
            pltpu.VMEM((chips, block, cols), bf16),
            pltpu.VMEM((max(na - 1, 1), nb, block, cols), bf16),
            pltpu.VMEM((max(nb - 1, 1), block, cols), bf16),
        ]
    scratch += [
        dma((micro, nw)), dma((micro, nw)), dma((micro, nw)), dma((micro, nw)),
        dma((micro,)), dma((micro,)),
        dma((3, micro, n - 1)), dma((3, micro, n - 1)),
        dma((2, chips)), dma((2, chips)),
        dma((2, top)), dma((2, top)), dma((2, top)), dma((2, top)),
    ]
    flops = 12 * micro * real * width * hidden
    outs = pl.pallas_call(
        functools.partial(kernel, sizes),
        out_shape=(
            shape((1, micro, rp, width), bf16),
            shape((1, micro, rp, width), bf16),
            shape((1, bi, hidden), f32),
            shape((1, bo, width), f32),
            shape((1, width), f32),
            shape((1, width), f32),
        ),
        in_specs=[vmem] * 6,
        out_specs=(vmem,) * 6,
        scratch_shapes=scratch,
        compiler_params=pltpu.CompilerParams(
            collective_id=0, has_side_effects=True, vmem_limit_bytes=60 * 1024 * 1024
        ),
        cost_estimate=pl.CostEstimate(
            flops=flops, bytes_accessed=8 * width * hidden, transcendentals=2 * micro * real * hidden
        ),
        name="relay",
    )(images, cotangent, w_in, w_out, gain, shift)
    return (outs[0][:, :, :real], outs[1][:, :, :real], *outs[2:])


def solution(mesh):
    placed = (
        P(None, "dp", None),
        P(None, "dp", None),
        P("section", None, None),
        P("section", None, None),
        P("section", None),
        P("section", None),
    )
    return jax.shard_map(
        local,
        mesh=mesh,
        in_specs=placed,
        out_specs=(
            P("section", None, "dp", None),
            P("section", None, "dp", None),
            P("section", "dp", None),
            P("section", "dp", None),
            P("section", None),
            P("section", None),
        ),
        check_vma=False,
    )
```

```python
import functools

import jax
import jax.numpy as jnp
from jax import lax
from jax.experimental import pallas as pl
from jax.experimental.pallas import tpu as pltpu
from jax.sharding import PartitionSpec as P

epsilon = 1e-05
gelu_scale = 0.7978845608028654
cubic_term = 0.044715
f32 = jnp.float32
bf16 = jnp.bfloat16
MESH = pl.DeviceIdType.MESH


def near_square(count):
    side = int(count**0.5)
    while count % side:
        side -= 1
    return side


def loop(count, body):
    def step(i, carry):
        body(i)
        return carry

    lax.fori_loop(0, count, step, 0)


def unrolled(count, body):
    for i in range(count):
        body(i)


def cut(j, size):
    if isinstance(j, int):
        return pl.ds(j * size, size)
    return pl.ds(pl.multiple_of(j * size, size), size)


def across(lhs, rhs):
    return lax.dot_general(lhs, rhs, (((1,), (1,)), ((), ())), preferred_element_type=f32)


def kernel(
    sizes,
    images, cotangent, w_in, w_out, gain, shift,
    out, gin, red_in, red_out, ggain, gshift,
    xbuf, ubuf, xout, uout, stat, stat_out, ex, aff, active, slope, gb, ga_buf, act_t, aff_t,
    send_i, keep_i, r0_i, r1_i, r2_i,
    send_o, keep_o, r0_o, r1_o, r2_o,
    x_send, x_recv, u_send, u_recv, st_send, st_recv, ex_send, ex_recv,
    s0, q0, s1, q1, s2, q2,
):
    sections, n, micro, real, rp, width, hidden, nx, ny = sizes
    rows = real * n
    wt = min(256, width)
    ht = min(512, hidden)
    nw = width // wt
    nh = hidden // ht
    section = lax.axis_index("section")
    me = lax.axis_index("dp")
    first = section == 0
    last = section == sections - 1
    not_first = section > 0
    not_last = section < sections - 1

    barrier = pltpu.get_barrier_semaphore()

    def greet(k):
        pl.semaphore_signal(
            barrier, inc=1, device_id={"dp": lax.rem(me + k + 1, n)}, device_id_type=MESH
        )

    loop(n - 1, greet)

    @pl.when(not_first)
    def _():
        pl.semaphore_signal(barrier, inc=1, device_id={"section": section - 1}, device_id_type=MESH)

    @pl.when(not_last)
    def _():
        pl.semaphore_signal(barrier, inc=1, device_id={"section": section + 1}, device_id_type=MESH)

    peers = n - 1 + not_first.astype(jnp.int32) + not_last.astype(jnp.int32)
    pl.semaphore_wait(barrier, peers)

    valid = lax.broadcasted_iota(jnp.int32, (rp, wt), 0) < real

    def local_stats(kind, m, j, tile):
        mean = jnp.sum(tile, axis=0, keepdims=True) / real
        gap = jnp.where(valid, tile - mean, 0.0)
        ex[kind, m, me, 0:1, cut(j, wt)] = mean
        ex[kind, m, me, 1:2, cut(j, wt)] = jnp.sum(gap * gap, axis=0, keepdims=True)

    def ex_copy(kind, m, k, slot):
        return pltpu.make_async_remote_copy(
            src_ref=ex.at[kind, m, slot],
            dst_ref=ex.at[kind, m, slot],
            send_sem=ex_send.at[kind, m, k],
            recv_sem=ex_recv.at[kind, m, k],
            device_id={"dp": lax.rem(me + k + 1, n)},
            device_id_type=MESH,
        )

    def ex_start(kind, m):
        loop(n - 1, lambda k: ex_copy(kind, m, k, me).start())

    def ex_wait(kind, m):
        loop(n - 1, lambda k: ex_copy(kind, m, k, lax.rem(me - k - 1 + n, n)).wait_recv())
        loop(n - 1, lambda k: ex_copy(kind, m, k, me).wait_send())
        return ex[kind, m]

    def combine(kind, m, target):
        parts = ex_wait(kind, m)
        means = parts[:, 0, :]
        mean = jnp.sum(means, axis=0, keepdims=True) / n
        gap = means - mean
        spread = (
            jnp.sum(parts[:, 1, :], axis=0, keepdims=True)
            + real * jnp.sum(gap * gap, axis=0, keepdims=True)
        ) / rows
        target[m, 0:1, :] = mean
        target[m, 1:2, :] = lax.rsqrt(spread + epsilon)

    def x_copy(m, j):
        return pltpu.make_async_remote_copy(
            src_ref=xout.at[m, :, cut(j, wt)],
            dst_ref=xbuf.at[m, :, cut(j, wt)],
            send_sem=x_send.at[m, j],
            recv_sem=x_recv.at[m, j],
            device_id={"section": section + 1},
            device_id_type=MESH,
        )

    def u_copy(m, j):
        return pltpu.make_async_remote_copy(
            src_ref=uout.at[m, :, cut(j, wt)],
            dst_ref=ubuf.at[m, :, cut(j, wt)],
            send_sem=u_send.at[m, j],
            recv_sem=u_recv.at[m, j],
            device_id={"section": section - 1},
            device_id_type=MESH,
        )

    def st_copy(m):
        return pltpu.make_async_remote_copy(
            src_ref=stat_out.at[m],
            dst_ref=stat.at[m],
            send_sem=st_send.at[m],
            recv_sem=st_recv.at[m],
            device_id={"section": section + 1},
            device_id_type=MESH,
        )

    ggain[...] = jnp.zeros_like(ggain)
    gshift[...] = jnp.zeros_like(gshift)

    @pl.when(first)
    def _():
        for m in range(micro):
            xbuf[m, rp - 16 : rp, :] = jnp.zeros((16, width), bf16)
            xbuf[m, 0:real, :] = images[m]

            def tile(j):
                local_stats(0, m, j, xbuf[m, :, cut(j, wt)].astype(f32))

            loop(nw, tile)
            ex_start(0, m)
        for m in range(micro):
            combine(0, m, stat)

    @pl.when(last)
    def _():
        for m in range(micro):
            ubuf[m, rp - 16 : rp, :] = jnp.zeros((16, width), bf16)
            ubuf[m, 0:real, :] = cotangent[m]

    def forward(m):
        @pl.when(not_first)
        def _():
            loop(nw, lambda j: x_copy(m, j).wait_recv())
            st_copy(m).wait_recv()

        mean = stat[m, 0:1, :]
        inverse = stat[m, 1:2, :]
        aff[m] = (
            (xbuf[m].astype(f32) - mean) * inverse * gain[...] + shift[...]
        ).astype(bf16)

        def hidden_tile(j):
            before = jnp.dot(aff[m], w_in[0, :, cut(j, ht)], preferred_element_type=f32)
            bend = jnp.tanh(gelu_scale * (before + cubic_term * before * before * before))
            active[m, :, cut(j, ht)] = (0.5 * before * (1.0 + bend)).astype(bf16)
            slope[m, :, cut(j, ht)] = before

        unrolled(nh, hidden_tile)

        def out_tile(j):
            fresh = xbuf[m, :, cut(j, wt)].astype(f32) + jnp.dot(
                active[m], w_out[0, :, cut(j, wt)], preferred_element_type=f32
            )
            fresh = jnp.where(valid, fresh, 0.0).astype(bf16)
            xout[m, :, cut(j, wt)] = fresh
            out[0, m, :, cut(j, wt)] = fresh[0:real]

            @pl.when(not_last)
            def _():
                x_copy(m, j).start()
                local_stats(1, m, j, fresh.astype(f32))

        loop(nw, out_tile)

        @pl.when(not_last)
        def _():
            ex_start(1, m)
            combine(1, m, stat_out)
            st_copy(m).start()

        def tail_tile(j):
            before = slope[m, :, cut(j, ht)]
            bend = jnp.tanh(gelu_scale * (before + cubic_term * before * before * before))
            slope[m, :, cut(j, ht)] = 0.5 * (1.0 + bend) + 0.5 * before * (
                1.0 - bend * bend
            ) * gelu_scale * (1.0 + 3.0 * cubic_term * before * before)
            act_t[m, cut(j, ht), :] = active[m, :, cut(j, ht)].T

        loop(nh, tail_tile)

        def turn_tile(j):
            aff_t[m, cut(j, wt), :] = aff[m, :, cut(j, wt)].T

        loop(nw, turn_tile)

    def receive(m):
        @pl.when(not_last)
        def _():
            loop(nw, lambda j: u_copy(m, j).wait_recv())

    def hidden_grad(m):
        def hidden_tile(j):
            pulled = across(ubuf[m], w_out[0, cut(j, ht), :])
            gb[m, :, cut(j, ht)] = (pulled * slope[m, :, cut(j, ht)]).astype(bf16)

        unrolled(nh, hidden_tile)

    def input_grad(m):
        def normed_of(j):
            return (
                xbuf[m, :, cut(j, wt)].astype(f32) - stat[m, 0:1, cut(j, wt)]
            ) * stat[m, 1:2, cut(j, wt)]

        def affine_tile(j):
            cols = cut(j, wt)
            pulled = across(gb[m], w_in[0, cols, :])
            ga_buf[:, cols] = pulled

            ex[2, m, me, 0:1, cols] = jnp.sum(pulled, axis=0, keepdims=True)
            ex[2, m, me, 1:2, cols] = jnp.sum(pulled * normed_of(j), axis=0, keepdims=True)

        unrolled(nw, affine_tile)
        ex_start(2, m)
        parts = ex_wait(2, m)
        sum_cross = jnp.sum(parts[:, 1, :], axis=0, keepdims=True)
        sum_grad = jnp.sum(parts[:, 0, :], axis=0, keepdims=True)

        ggain[...] += sum_cross
        gshift[...] += sum_grad

        def grad_tile(j):
            cols = cut(j, wt)
            sums = ex[2, m, :, :, cols]
            part_grad = jnp.sum(sums[:, 0, :], axis=0, keepdims=True)
            part_cross = jnp.sum(sums[:, 1, :], axis=0, keepdims=True)
            fresh = ubuf[m, :, cols].astype(f32) + stat[m, 1:2, cols] * gain[:, cols] * (
                ga_buf[:, cols] - part_grad / rows - normed_of(j) * (part_cross / rows)
            )
            fresh = jnp.where(valid, fresh, 0.0).astype(bf16)
            uout[m, :, cols] = fresh

            @pl.when(not_first)
            def _():
                u_copy(m, j).start()

            gin[0, m, :, cols] = fresh[0:real]

        loop(nw, grad_tile)

    def backward(m):
        receive(m)
        hidden_grad(m)
        input_grad(m)

    def step(t):
        ahead = jnp.where(last, lax.rem(t, 2) == 0, t < micro)
        m = jnp.where(last, t // 2, lax.rem(t, micro))

        @pl.when(ahead)
        def _():
            forward(m)

        @pl.when(jnp.logical_not(ahead))
        def _():
            backward(m)

    loop(2 * micro - 1, step)

    core = lax.rem(me, 2)
    chip = me // 2
    my_y = chip // nx
    my_x = lax.rem(chip, nx)

    def place(y, x, c):
        return (y * nx + x) * 2 + c

    plans = (
        (0, ny, nx, my_y, my_x, lambda a, b, c: place(a, b, c), act_t, ubuf,
         send_o, keep_o, r0_o, r1_o, r2_o, red_out, hidden // n),
        (1, nx, ny, my_x, my_y, lambda a, b, c: place(b, a, c), aff_t, gb,
         send_i, keep_i, r0_i, r1_i, r2_i, red_in, width // n),
    )

    def copy0(g, plan, s):
        return pltpu.make_async_remote_copy(
            src_ref=plan[8].at[s], dst_ref=plan[10].at[s],
            send_sem=s0.at[g, s], recv_sem=q0.at[g, s],
            device_id={"dp": chip * 2 + 1 - core}, device_id_type=MESH,
        )

    def copy1(g, plan, k, slot):
        na, nb, a, b, where = plan[1:6]
        to = lax.rem(a + k + 1, na)
        return pltpu.make_async_remote_copy(
            src_ref=plan[8].at[pl.ds(to * nb, nb)], dst_ref=plan[11].at[k],
            send_sem=s1.at[g, k], recv_sem=q1.at[g, k],
            device_id={"dp": where(to, b, core)}, device_id_type=MESH,
        )

    def copy2(g, plan, k):
        na, nb, a, b, where = plan[1:6]
        to = lax.rem(b + k + 1, nb)
        return pltpu.make_async_remote_copy(
            src_ref=plan[8].at[a * nb + to], dst_ref=plan[12].at[k],
            send_sem=s2.at[g, k], recv_sem=q2.at[g, k],
            device_id={"dp": where(a, to, core)}, device_id_type=MESH,
        )

    def partial(plan, owner):
        left, right, block = plan[6], plan[7], plan[14]
        total = jnp.dot(left[0, cut(owner, block), :], right[0], preferred_element_type=f32)
        for m in range(1, micro):
            total += jnp.dot(left[m, cut(owner, block), :], right[m], preferred_element_type=f32)
        return total

    def send_away(plan):
        g, na, nb, a, b, where = plan[:6]
        send = plan[8]

        def away(s):
            owner = where(s // nb, lax.rem(s, nb), 1 - core)
            send[s] = partial(plan, owner).astype(bf16)
            copy0(g, plan, s).start()

        loop(na * nb, away)

    def send_first(plan):
        g, na, nb, a, b, where, left, right, send, keep, r0, r1, r2, red, block = plan

        def other(k):
            to = lax.rem(a + k + 1, na)

            def one(i):
                s = to * nb + i
                total = partial(plan, where(to, i, core))
                copy0(g, plan, s).wait()
                send[s] = (total + r0[s].astype(f32)).astype(bf16)

            loop(nb, one)
            copy1(g, plan, k, 0).start()

        loop(na - 1, other)

    def own_first(plan):
        g, na, nb, a, b, where, left, right, send, keep, r0, r1, r2, red, block = plan

        def own(i):
            s = a * nb + i
            total = partial(plan, where(a, i, core))
            copy0(g, plan, s).wait()
            keep[i] = total + r0[s].astype(f32)

        loop(nb, own)

    final = micro - 1
    receive(final)

    @pl.when(first)
    def _():
        send_away(plans[0])

    hidden_grad(final)

    @pl.when(first)
    def _():
        send_away(plans[1])
        send_first(plans[0])
        send_first(plans[1])

    input_grad(final)

    @pl.when(not_first)
    def _():
        send_away(plans[0])
        send_away(plans[1])
        send_first(plans[0])
        send_first(plans[1])

    own_first(plans[0])
    own_first(plans[1])

    for plan in plans:
        g, na, nb, a, b, where, left, right, send, keep, r0, r1, r2, red, block = plan
        loop(na - 1, lambda k: copy1(g, plan, k, 0).wait())

        def across_sum(to):
            total = keep[to]
            for k in range(na - 1):
                total += r1[k, to].astype(f32)
            return total

        def other2(k):
            to = lax.rem(b + k + 1, nb)
            send[a * nb + to] = across_sum(to).astype(bf16)
            copy2(g, plan, k).start()

        loop(nb - 1, other2)
        keep[b] = across_sum(b)

    for plan in plans:
        g, na, nb, a, b, where, left, right, send, keep, r0, r1, r2, red, block = plan
        loop(nb - 1, lambda k: copy2(g, plan, k).wait())
        total = keep[b]
        for k in range(nb - 1):
            total += r2[k].astype(f32)
        red[0] = total

    @pl.when(not_last)
    def _():
        for m in range(micro):
            loop(nw, lambda j: x_copy(m, j).wait_send())
            st_copy(m).wait_send()

    @pl.when(not_first)
    def _():
        for m in range(micro):
            loop(nw, lambda j: u_copy(m, j).wait_send())


def local(images, cotangent, w_in, w_out, gain, shift):
    sections = lax.axis_size("section")
    n = lax.axis_size("dp")
    micro, real, width = images.shape
    hidden = w_in.shape[2]
    rp = -(-real // 16) * 16
    chips = n // 2
    ny = near_square(chips)
    nx = chips // ny
    nw = width // min(256, width)
    bi, bo = width // n, hidden // n
    top = max(nx, ny)
    sizes = (sections, n, micro, real, rp, width, hidden, nx, ny)
    shape = jax.ShapeDtypeStruct
    vmem = pl.BlockSpec(memory_space=pltpu.VMEM)
    dma = pltpu.SemaphoreType.DMA
    scratch = [
        pltpu.VMEM((micro, rp, width), bf16),
        pltpu.VMEM((micro, rp, width), bf16),
        pltpu.VMEM((micro, rp, width), bf16),
        pltpu.VMEM((micro, rp, width), bf16),
        pltpu.VMEM((micro, 2, width), f32),
        pltpu.VMEM((micro, 2, width), f32),
        pltpu.VMEM((3, micro, n, 2, width), f32),
        pltpu.VMEM((micro, rp, width), bf16),
        pltpu.VMEM((micro, rp, hidden), bf16),
        pltpu.VMEM((micro, rp, hidden), f32),
        pltpu.VMEM((micro, rp, hidden), bf16),
        pltpu.VMEM((rp, width), f32),
        pltpu.VMEM((micro, hidden, rp), bf16),
        pltpu.VMEM((micro, width, rp), bf16),
    ]
    for na, nb, block, cols in ((nx, ny, bi, hidden), (ny, nx, bo, width)):
        scratch += [
            pltpu.VMEM((chips, block, cols), bf16),
            pltpu.VMEM((nb, block, cols), f32),
            pltpu.VMEM((chips, block, cols), bf16),
            pltpu.VMEM((max(na - 1, 1), nb, block, cols), bf16),
            pltpu.VMEM((max(nb - 1, 1), block, cols), bf16),
        ]
    scratch += [
        dma((micro, nw)), dma((micro, nw)), dma((micro, nw)), dma((micro, nw)),
        dma((micro,)), dma((micro,)),
        dma((3, micro, n - 1)), dma((3, micro, n - 1)),
        dma((2, chips)), dma((2, chips)),
        dma((2, top)), dma((2, top)), dma((2, top)), dma((2, top)),
    ]
    flops = 12 * micro * real * width * hidden
    outs = pl.pallas_call(
        functools.partial(kernel, sizes),
        out_shape=(
            shape((1, micro, real, width), bf16),
            shape((1, micro, real, width), bf16),
            shape((1, bi, hidden), f32),
            shape((1, bo, width), f32),
            shape((1, width), f32),
            shape((1, width), f32),
        ),
        in_specs=[vmem] * 6,
        out_specs=(vmem,) * 6,
        scratch_shapes=scratch,
        compiler_params=pltpu.CompilerParams(
            collective_id=0, has_side_effects=True, vmem_limit_bytes=60 * 1024 * 1024
        ),
        cost_estimate=pl.CostEstimate(
            flops=flops, bytes_accessed=8 * width * hidden, transcendentals=2 * micro * real * hidden
        ),
        name="relay",
    )(images, cotangent, w_in, w_out, gain, shift)
    return tuple(outs)


def solution(mesh):
    placed = (
        P(None, "dp", None),
        P(None, "dp", None),
        P("section", None, None),
        P("section", None, None),
        P("section", None),
        P("section", None),
    )
    return jax.shard_map(
        local,
        mesh=mesh,
        in_specs=placed,
        out_specs=(
            P("section", None, "dp", None),
            P("section", None, "dp", None),
            P("section", "dp", None),
            P("section", "dp", None),
            P("section", None),
            P("section", None),
        ),
        check_vma=False,
    )
```

```python
import functools

import jax
import jax.numpy as jnp
from jax import lax
from jax.experimental import pallas as pl
from jax.experimental.pallas import tpu as pltpu
from jax.sharding import PartitionSpec as P

epsilon = 1e-05
gelu_scale = 0.7978845608028654
cubic_term = 0.044715
f32 = jnp.float32
bf16 = jnp.bfloat16
MESH = pl.DeviceIdType.MESH


def near_square(count):
    side = int(count**0.5)
    while count % side:
        side -= 1
    return side


def loop(count, body):
    def step(i, carry):
        body(i)
        return carry

    lax.fori_loop(0, count, step, 0)


def unrolled(count, body):
    for i in range(count):
        body(i)


def cut(j, size):
    if isinstance(j, int):
        return pl.ds(j * size, size)
    return pl.ds(pl.multiple_of(j * size, size), size)


def across(lhs, rhs):
    return lax.dot_general(lhs, rhs, (((1,), (1,)), ((), ())), preferred_element_type=f32)


def kernel(
    sizes,
    images, cotangent, w_in, w_out, gain, shift,
    out, gin, red_in, red_out, ggain, gshift,
    xbuf, ubuf, xout, uout, stat, stat_out, ex, aff, active, slope, gb, ga_buf, act_t, aff_t,
    send_i, keep_i, r0_i, r1_i, r2_i,
    send_o, keep_o, r0_o, r1_o, r2_o,
    x_send, x_recv, u_send, u_recv, st_send, st_recv, ex_send, ex_recv,
    s0, q0, s1, q1, s2, q2,
):
    sections, n, micro, real, rp, width, hidden, nx, ny = sizes
    rows = real * n
    wt = min(256, width)
    ht = min(512, hidden)
    nw = width // wt
    nh = hidden // ht
    section = lax.axis_index("section")
    me = lax.axis_index("dp")
    first = section == 0
    last = section == sections - 1
    not_first = section > 0
    not_last = section < sections - 1

    barrier = pltpu.get_barrier_semaphore()

    def greet(k):
        pl.semaphore_signal(
            barrier, inc=1, device_id={"dp": lax.rem(me + k + 1, n)}, device_id_type=MESH
        )

    loop(n - 1, greet)

    @pl.when(not_first)
    def _():
        pl.semaphore_signal(barrier, inc=1, device_id={"section": section - 1}, device_id_type=MESH)

    @pl.when(not_last)
    def _():
        pl.semaphore_signal(barrier, inc=1, device_id={"section": section + 1}, device_id_type=MESH)

    peers = n - 1 + not_first.astype(jnp.int32) + not_last.astype(jnp.int32)
    pl.semaphore_wait(barrier, peers)

    valid = lax.broadcasted_iota(jnp.int32, (rp, wt), 0) < real

    def local_stats(kind, m, j, tile):
        mean = jnp.sum(tile, axis=0, keepdims=True) / real
        gap = jnp.where(valid, tile - mean, 0.0)
        ex[kind, m, me, 0:1, cut(j, wt)] = mean
        ex[kind, m, me, 1:2, cut(j, wt)] = jnp.sum(gap * gap, axis=0, keepdims=True)

    def ex_copy(kind, m, k, slot):
        return pltpu.make_async_remote_copy(
            src_ref=ex.at[kind, m, slot],
            dst_ref=ex.at[kind, m, slot],
            send_sem=ex_send.at[kind, m, k],
            recv_sem=ex_recv.at[kind, m, k],
            device_id={"dp": lax.rem(me + k + 1, n)},
            device_id_type=MESH,
        )

    def ex_start(kind, m):
        loop(n - 1, lambda k: ex_copy(kind, m, k, me).start())

    def ex_wait(kind, m):
        loop(n - 1, lambda k: ex_copy(kind, m, k, lax.rem(me - k - 1 + n, n)).wait_recv())
        loop(n - 1, lambda k: ex_copy(kind, m, k, me).wait_send())
        return ex[kind, m]

    def combine(kind, m, target):
        parts = ex_wait(kind, m)
        means = parts[:, 0, :]
        mean = jnp.sum(means, axis=0, keepdims=True) / n
        gap = means - mean
        spread = (
            jnp.sum(parts[:, 1, :], axis=0, keepdims=True)
            + real * jnp.sum(gap * gap, axis=0, keepdims=True)
        ) / rows
        target[m, 0:1, :] = mean
        target[m, 1:2, :] = lax.rsqrt(spread + epsilon)

    def x_copy(m, j):
        return pltpu.make_async_remote_copy(
            src_ref=xout.at[m, :, cut(j, wt)],
            dst_ref=xbuf.at[m, :, cut(j, wt)],
            send_sem=x_send.at[m, j],
            recv_sem=x_recv.at[m, j],
            device_id={"section": section + 1},
            device_id_type=MESH,
        )

    def u_copy(m, j):
        return pltpu.make_async_remote_copy(
            src_ref=uout.at[m, :, cut(j, wt)],
            dst_ref=ubuf.at[m, :, cut(j, wt)],
            send_sem=u_send.at[m, j],
            recv_sem=u_recv.at[m, j],
            device_id={"section": section - 1},
            device_id_type=MESH,
        )

    def st_copy(m):
        return pltpu.make_async_remote_copy(
            src_ref=stat_out.at[m],
            dst_ref=stat.at[m],
            send_sem=st_send.at[m],
            recv_sem=st_recv.at[m],
            device_id={"section": section + 1},
            device_id_type=MESH,
        )

    ggain[...] = jnp.zeros_like(ggain)
    gshift[...] = jnp.zeros_like(gshift)

    @pl.when(first)
    def _():
        for m in range(micro):
            xbuf[m, rp - 16 : rp, :] = jnp.zeros((16, width), bf16)
            xbuf[m, 0:real, :] = images[:, m, :]

            def tile(j):
                local_stats(0, m, j, xbuf[m, :, cut(j, wt)].astype(f32))

            loop(nw, tile)
            ex_start(0, m)
        for m in range(micro):
            combine(0, m, stat)

    @pl.when(last)
    def _():
        for m in range(micro):
            ubuf[m, rp - 16 : rp, :] = jnp.zeros((16, width), bf16)
            ubuf[m, 0:real, :] = cotangent[:, m, :]

    def forward(m):
        @pl.when(not_first)
        def _():
            loop(nw, lambda j: x_copy(m, j).wait_recv())
            st_copy(m).wait_recv()

        mean = stat[m, 0:1, :]
        inverse = stat[m, 1:2, :]
        aff[m] = (
            (xbuf[m].astype(f32) - mean) * inverse * gain[...] + shift[...]
        ).astype(bf16)

        def hidden_tile(j):
            before = jnp.dot(aff[m], w_in[0, :, cut(j, ht)], preferred_element_type=f32)
            bend = jnp.tanh(gelu_scale * (before + cubic_term * before * before * before))
            active[m, :, cut(j, ht)] = (0.5 * before * (1.0 + bend)).astype(bf16)
            slope[m, :, cut(j, ht)] = before

        unrolled(nh, hidden_tile)

        def out_tile(j):
            fresh = xbuf[m, :, cut(j, wt)].astype(f32) + jnp.dot(
                active[m], w_out[0, :, cut(j, wt)], preferred_element_type=f32
            )
            fresh = jnp.where(valid, fresh, 0.0).astype(bf16)
            xout[m, :, cut(j, wt)] = fresh
            out[0, m, :, cut(j, wt)] = fresh[0:real]

            @pl.when(not_last)
            def _():
                x_copy(m, j).start()
                local_stats(1, m, j, fresh.astype(f32))

        loop(nw, out_tile)

        @pl.when(not_last)
        def _():
            ex_start(1, m)
            combine(1, m, stat_out)
            st_copy(m).start()

        def tail_tile(j):
            before = slope[m, :, cut(j, ht)]
            bend = jnp.tanh(gelu_scale * (before + cubic_term * before * before * before))
            slope[m, :, cut(j, ht)] = 0.5 * (1.0 + bend) + 0.5 * before * (
                1.0 - bend * bend
            ) * gelu_scale * (1.0 + 3.0 * cubic_term * before * before)

        loop(nh, tail_tile)

        @pl.when(not_last)
        def _():
            turn(m)

    def turn(m):
        def active_tile(j):
            act_t[m, cut(j, ht), :] = active[m, :, cut(j, ht)].T

        loop(nh, active_tile)

        def affine_tile(j):
            aff_t[m, cut(j, wt), :] = aff[m, :, cut(j, wt)].T

        loop(nw, affine_tile)

    def receive(m):
        @pl.when(not_last)
        def _():
            loop(nw, lambda j: u_copy(m, j).wait_recv())

    def hidden_grad(m):
        def hidden_tile(j):
            pulled = across(ubuf[m], w_out[0, cut(j, ht), :])
            gb[m, :, cut(j, ht)] = (pulled * slope[m, :, cut(j, ht)]).astype(bf16)

        unrolled(nh, hidden_tile)

    def input_grad(m):
        def normed_of(j):
            return (
                xbuf[m, :, cut(j, wt)].astype(f32) - stat[m, 0:1, cut(j, wt)]
            ) * stat[m, 1:2, cut(j, wt)]

        def affine_tile(j):
            cols = cut(j, wt)
            pulled = across(gb[m], w_in[0, cols, :])
            ga_buf[:, cols] = pulled

            ex[2, m, me, 0:1, cols] = jnp.sum(pulled, axis=0, keepdims=True)
            ex[2, m, me, 1:2, cols] = jnp.sum(pulled * normed_of(j), axis=0, keepdims=True)

        unrolled(nw, affine_tile)
        ex_start(2, m)
        parts = ex_wait(2, m)
        sum_cross = jnp.sum(parts[:, 1, :], axis=0, keepdims=True)
        sum_grad = jnp.sum(parts[:, 0, :], axis=0, keepdims=True)

        ggain[...] += sum_cross
        gshift[...] += sum_grad

        def grad_tile(j):
            cols = cut(j, wt)
            sums = ex[2, m, :, :, cols]
            part_grad = jnp.sum(sums[:, 0, :], axis=0, keepdims=True)
            part_cross = jnp.sum(sums[:, 1, :], axis=0, keepdims=True)
            fresh = ubuf[m, :, cols].astype(f32) + stat[m, 1:2, cols] * gain[:, cols] * (
                ga_buf[:, cols] - part_grad / rows - normed_of(j) * (part_cross / rows)
            )
            fresh = jnp.where(valid, fresh, 0.0).astype(bf16)
            uout[m, :, cols] = fresh

            @pl.when(not_first)
            def _():
                u_copy(m, j).start()

            gin[0, m, :, cols] = fresh[0:real]

        loop(nw, grad_tile)

    def backward(m):
        receive(m)
        hidden_grad(m)
        input_grad(m)

        @pl.when(last)
        def _():
            turn(m)

    def step(t):
        ahead = jnp.where(last, lax.rem(t, 2) == 0, t < micro)
        m = jnp.where(last, t // 2, lax.rem(t, micro))

        @pl.when(ahead)
        def _():
            forward(m)

        @pl.when(jnp.logical_not(ahead))
        def _():
            backward(m)

    loop(2 * micro - 1, step)

    core = lax.rem(me, 2)
    chip = me // 2
    my_y = chip // nx
    my_x = lax.rem(chip, nx)

    def place(y, x, c):
        return (y * nx + x) * 2 + c

    plans = (
        (0, ny, nx, my_y, my_x, lambda a, b, c: place(a, b, c), act_t, ubuf,
         send_o, keep_o, r0_o, r1_o, r2_o, red_out, hidden // n),
        (1, nx, ny, my_x, my_y, lambda a, b, c: place(b, a, c), aff_t, gb,
         send_i, keep_i, r0_i, r1_i, r2_i, red_in, width // n),
    )

    def copy0(g, plan, s):
        return pltpu.make_async_remote_copy(
            src_ref=plan[8].at[s], dst_ref=plan[10].at[s],
            send_sem=s0.at[g, s], recv_sem=q0.at[g, s],
            device_id={"dp": chip * 2 + 1 - core}, device_id_type=MESH,
        )

    def copy1(g, plan, k, slot):
        na, nb, a, b, where = plan[1:6]
        to = lax.rem(a + k + 1, na)
        return pltpu.make_async_remote_copy(
            src_ref=plan[8].at[pl.ds(to * nb, nb)], dst_ref=plan[11].at[k],
            send_sem=s1.at[g, k], recv_sem=q1.at[g, k],
            device_id={"dp": where(to, b, core)}, device_id_type=MESH,
        )

    def copy2(g, plan, k):
        na, nb, a, b, where = plan[1:6]
        to = lax.rem(b + k + 1, nb)
        return pltpu.make_async_remote_copy(
            src_ref=plan[8].at[a * nb + to], dst_ref=plan[12].at[k],
            send_sem=s2.at[g, k], recv_sem=q2.at[g, k],
            device_id={"dp": where(a, to, core)}, device_id_type=MESH,
        )

    def partial(plan, owner):
        left, right, block = plan[6], plan[7], plan[14]
        total = jnp.dot(left[0, cut(owner, block), :], right[0], preferred_element_type=f32)
        for m in range(1, micro):
            total += jnp.dot(left[m, cut(owner, block), :], right[m], preferred_element_type=f32)
        return total

    def send_away(plan):
        g, na, nb, a, b, where = plan[:6]
        send = plan[8]

        def away(s):
            owner = where(s // nb, lax.rem(s, nb), 1 - core)
            send[s] = partial(plan, owner).astype(bf16)
            copy0(g, plan, s).start()

        loop(na * nb, away)

    def send_first(plan):
        g, na, nb, a, b, where, left, right, send, keep, r0, r1, r2, red, block = plan

        def other(k):
            to = lax.rem(a + k + 1, na)

            def one(i):
                s = to * nb + i
                total = partial(plan, where(to, i, core))
                copy0(g, plan, s).wait()
                send[s] = (total + r0[s].astype(f32)).astype(bf16)

            loop(nb, one)
            copy1(g, plan, k, 0).start()

        loop(na - 1, other)

    def own_first(plan):
        g, na, nb, a, b, where, left, right, send, keep, r0, r1, r2, red, block = plan

        def own(i):
            s = a * nb + i
            total = partial(plan, where(a, i, core))
            copy0(g, plan, s).wait()
            keep[i] = total + r0[s].astype(f32)

        loop(nb, own)

    final = micro - 1
    receive(final)

    @pl.when(first)
    def _():
        send_away(plans[0])

    hidden_grad(final)

    @pl.when(first)
    def _():
        send_away(plans[1])
        send_first(plans[0])
        send_first(plans[1])

    input_grad(final)

    @pl.when(last)
    def _():
        turn(final)

    @pl.when(not_first)
    def _():
        send_away(plans[0])
        send_away(plans[1])
        send_first(plans[0])
        send_first(plans[1])

    own_first(plans[0])
    own_first(plans[1])

    for plan in plans:
        g, na, nb, a, b, where, left, right, send, keep, r0, r1, r2, red, block = plan
        loop(na - 1, lambda k: copy1(g, plan, k, 0).wait())

        def across_sum(to):
            total = keep[to]
            for k in range(na - 1):
                total += r1[k, to].astype(f32)
            return total

        def other2(k):
            to = lax.rem(b + k + 1, nb)
            send[a * nb + to] = across_sum(to).astype(bf16)
            copy2(g, plan, k).start()

        loop(nb - 1, other2)
        keep[b] = across_sum(b)

    for plan in plans:
        g, na, nb, a, b, where, left, right, send, keep, r0, r1, r2, red, block = plan
        loop(nb - 1, lambda k: copy2(g, plan, k).wait())
        total = keep[b]
        for k in range(nb - 1):
            total += r2[k].astype(f32)
        red[0] = total

    @pl.when(not_last)
    def _():
        for m in range(micro):
            loop(nw, lambda j: x_copy(m, j).wait_send())
            st_copy(m).wait_send()

    @pl.when(not_first)
    def _():
        for m in range(micro):
            loop(nw, lambda j: u_copy(m, j).wait_send())


def local(images, cotangent, w_in, w_out, gain, shift):
    sections = lax.axis_size("section")
    n = lax.axis_size("dp")
    micro, real, width = images.shape
    hidden = w_in.shape[2]
    rp = -(-real // 16) * 16
    chips = n // 2
    ny = near_square(chips)
    nx = chips // ny
    nw = width // min(256, width)
    bi, bo = width // n, hidden // n
    top = max(nx, ny)
    sizes = (sections, n, micro, real, rp, width, hidden, nx, ny)
    shape = jax.ShapeDtypeStruct
    vmem = pl.BlockSpec(memory_space=pltpu.VMEM)
    dma = pltpu.SemaphoreType.DMA
    scratch = [
        pltpu.VMEM((micro, rp, width), bf16),
        pltpu.VMEM((micro, rp, width), bf16),
        pltpu.VMEM((micro, rp, width), bf16),
        pltpu.VMEM((micro, rp, width), bf16),
        pltpu.VMEM((micro, 2, width), f32),
        pltpu.VMEM((micro, 2, width), f32),
        pltpu.VMEM((3, micro, n, 2, width), f32),
        pltpu.VMEM((micro, rp, width), bf16),
        pltpu.VMEM((micro, rp, hidden), bf16),
        pltpu.VMEM((micro, rp, hidden), f32),
        pltpu.VMEM((micro, rp, hidden), bf16),
        pltpu.VMEM((rp, width), f32),
        pltpu.VMEM((micro, hidden, rp), bf16),
        pltpu.VMEM((micro, width, rp), bf16),
    ]
    for na, nb, block, cols in ((nx, ny, bi, hidden), (ny, nx, bo, width)):
        scratch += [
            pltpu.VMEM((chips, block, cols), bf16),
            pltpu.VMEM((nb, block, cols), f32),
            pltpu.VMEM((chips, block, cols), bf16),
            pltpu.VMEM((max(na - 1, 1), nb, block, cols), bf16),
            pltpu.VMEM((max(nb - 1, 1), block, cols), bf16),
        ]
    scratch += [
        dma((micro, nw)), dma((micro, nw)), dma((micro, nw)), dma((micro, nw)),
        dma((micro,)), dma((micro,)),
        dma((3, micro, n - 1)), dma((3, micro, n - 1)),
        dma((2, chips)), dma((2, chips)),
        dma((2, top)), dma((2, top)), dma((2, top)), dma((2, top)),
    ]
    flops = 12 * micro * real * width * hidden
    outs = pl.pallas_call(
        functools.partial(kernel, sizes),
        out_shape=(
            shape((1, micro, real, width), bf16),
            shape((1, micro, real, width), bf16),
            shape((1, bi, hidden), f32),
            shape((1, bo, width), f32),
            shape((1, width), f32),
            shape((1, width), f32),
        ),
        in_specs=[vmem] * 6,
        out_specs=(vmem,) * 6,
        scratch_shapes=scratch,
        compiler_params=pltpu.CompilerParams(
            collective_id=0, has_side_effects=True, vmem_limit_bytes=60 * 1024 * 1024
        ),
        cost_estimate=pl.CostEstimate(
            flops=flops, bytes_accessed=8 * width * hidden, transcendentals=2 * micro * real * hidden
        ),
        name="relay",
    )(jnp.swapaxes(images, 0, 1), jnp.swapaxes(cotangent, 0, 1), w_in, w_out, gain, shift)
    return tuple(outs)


def solution(mesh):
    placed = (
        P(None, "dp", None),
        P(None, "dp", None),
        P("section", None, None),
        P("section", None, None),
        P("section", None),
        P("section", None),
    )
    return jax.shard_map(
        local,
        mesh=mesh,
        in_specs=placed,
        out_specs=(
            P("section", None, "dp", None),
            P("section", None, "dp", None),
            P("section", "dp", None),
            P("section", "dp", None),
            P("section", None),
            P("section", None),
        ),
        check_vma=False,
    )
```
